512 devices in a mesh: ctx: 32 (over x, y, core), head: 16 (over z).
Axes of the slice: x: 4, y: 4, z: 16, core: 2. Of those that a mesh axis runs over, the one named last changes fastest.
Arguments:
- tokens: bfloat16 [4096, 4096], P('ctx', 'head'), may hold values from -6 to 6
- w_query: bfloat16 [4096, 2048], P(None, 'head'), may hold values from -0.09375 to 0.09375
- w_key: bfloat16 [4096, 2048], P(None, 'head'), may hold values from -0.09375 to 0.09375
- w_value: bfloat16 [4096, 2048], P(None, 'head'), may hold values from -0.09375 to 0.09375
- w_beta: bfloat16 [4096, 16], P(None, 'head'), may hold values from -0.046875 to 0.046875
- beta_bias: float32 [16], P('head'), may hold values from -4.6 to 2, as said below
- w_out: bfloat16 [2048, 4096], P('head'), may hold values from -0.125 to 0.125
Outputs:
- mixed_out: bfloat16 [4096, 4096], P('ctx', 'head')
The draws below stay inside these ranges and needn't reach their ends.
Inputs may be any that keep to these rules, and one draw needn't show every extreme that they name: `beta_bias`: one bias for each head.
All inputs are finite; a program needn't handle non-finite values.
Results may differ from the reference program's by a relative error of at most 0.025.
Values may be sent and summed in bfloat16 or wider, within the bound.
A program may use at most 64 MiB of HBM per device.

```python
import jax
import jax.numpy as jnp
from jax import lax

D = 4096
DK = 128
DV = 128
HEADS_DEV = 1
HEADS = 16
SPAN = 128
SEQ = 4096
N_HEAD = 16


def draw_beta_bias(key, part):
    key = jax.random.fold_in(key, 5)
    first, second, third = jax.random.split(key, 3)
    slow = jax.random.uniform(first, (HEADS,), jnp.float32, -4.6, -4.0)
    fast = jax.random.uniform(second, (HEADS,), jnp.float32, 0.0, 2.0)
    order = jax.random.permutation(third, HEADS)
    cutoff = HEADS // 2
    return jnp.where(order < cutoff, fast, slow).astype(jnp.float32)


def shard_levels(stream_key, extent, pieces, least, top_value):
    loudness, own = 1.0, jax.random.fold_in(stream_key, 6)
    for axis_at, parts in pieces:
        heights = jnp.exp(jax.random.uniform(jax.random.fold_in(own, axis_at), (parts,), jnp.float32, least / len(pieces), top_value / len(pieces)))
        loudness = loudness * jnp.repeat(heights, extent[axis_at] // parts).reshape([-1 if axis == axis_at else 1 for axis in range(len(extent))])
    return loudness


def bell_draw(key, shape, scale, limit, cuts=(), kind=jnp.bfloat16):
    factor_of = shard_levels(key, shape, cuts, -0.22, 0.18) if cuts else 1.0
    array = jax.random.normal(key, shape, jnp.float32) * scale * factor_of
    return jnp.minimum(jnp.maximum(array, -limit), limit).astype(kind)


def setup_inputs(seed: int = 0) -> dict:
    keys = jax.random.split(jax.random.key(seed), 8)
    tokens = bell_draw(keys[0], (SEQ, D), 1.0, 6.0, ((0, 32), (1, 16)))
    w_query = bell_draw(keys[1], (D, HEADS * DK), D ** -0.5, 0.09375, ((1, 16),))
    w_key = bell_draw(keys[2], (D, HEADS * DK), D ** -0.5, 0.09375, ((1, 16),))
    w_value = bell_draw(keys[3], (D, HEADS * DV), D ** -0.5, 0.09375, ((1, 16),))
    w_beta = bell_draw(keys[4], (D, HEADS), (4 * D) ** -0.5, 0.046875, ((1, 16),))
    beta_bias = draw_beta_bias(jax.random.fold_in(keys[7], 71), 0)
    w_out = bell_draw(keys[6], (HEADS * DV, D), (HEADS * DV) ** -0.5, 0.125, ((0, 16),))
    return {"tokens": tokens, "w_query": w_query, "w_key": w_key, "w_value": w_value, "w_beta": w_beta, "beta_bias": beta_bias, "w_out": w_out}


highest = lax.Precision.HIGHEST

def unit_rows(matrix):
    return matrix / jnp.sqrt(lax.optimization_barrier(jnp.sum(matrix * matrix, axis=-1, keepdims=True)) + 1e-06)

def lower_solve(system, right_side):
    return lax.linalg.triangular_solve(system, right_side, left_side=True, lower=True, unit_diagonal=True)

def head_run(query_rows, key_rows, value_rows, beta_rows):
    count = query_rows.shape[0] // SPAN
    strict = jnp.tril(jnp.ones((SPAN, SPAN), jnp.float32), -1)
    eye_block = jnp.eye(SPAN, dtype=jnp.float32)

    def advance(state, block):
        query_block, key_block, value_block, beta_block = block
        inner = jnp.dot(key_block, key_block.T, precision=highest)
        system = eye_block + strict * beta_block[:, None] * inner
        weighted = lower_solve(system, beta_block[:, None] * key_block)
        updates = lower_solve(system, beta_block[:, None] * value_block)
        causal = jnp.tril(jnp.dot(query_block, key_block.T, precision=highest))
        fresh = updates - jnp.dot(weighted, state, precision=highest)
        output = jnp.dot(query_block, state, precision=highest) + jnp.dot(causal, fresh, precision=highest)
        state = state + jnp.dot(key_block.T, fresh, precision=highest)
        return (state, output)
    blocks = (query_rows.reshape(count, SPAN, DK), key_rows.reshape(count, SPAN, DK), value_rows.reshape(count, SPAN, DV), beta_rows.reshape(count, SPAN))
    final_state, outputs = lax.scan(advance, jnp.zeros((DK, DV), jnp.float32), blocks)
    return outputs.reshape(count * SPAN, DV)

def reference(tokens, w_query, w_key, w_value, w_beta, beta_bias, w_out):
    length = tokens.shape[0]
    query = unit_rows(jnp.dot(tokens.astype(jnp.float32), w_query.astype(jnp.float32), preferred_element_type=jnp.float32).reshape(length, HEADS, DK))
    key_all = unit_rows(jnp.dot(tokens.astype(jnp.float32), w_key.astype(jnp.float32), preferred_element_type=jnp.float32).reshape(length, HEADS, DK))
    value = jnp.dot(tokens.astype(jnp.float32), w_value.astype(jnp.float32), preferred_element_type=jnp.float32).reshape(length, HEADS, DV)
    beta = jax.nn.sigmoid(jnp.dot(tokens.astype(jnp.float32), w_beta.astype(jnp.float32), preferred_element_type=jnp.float32) + beta_bias)
    attended = jax.vmap(head_run, in_axes=1, out_axes=1)(query, key_all, value, beta)
    attended = attended.reshape(length, HEADS * DV).astype(jnp.bfloat16)
    group = HEADS_DEV * DV

    def add_group(index, total):
        offset = (index * group).astype(jnp.int32)
        piece = lax.dynamic_slice_in_dim(attended, offset, group, 1)
        weight_rows = lax.dynamic_slice_in_dim(w_out, offset, group, 0)
        partial_value = jnp.dot(piece.astype(jnp.float32), weight_rows.astype(jnp.float32), preferred_element_type=jnp.float32).astype(jnp.bfloat16)
        partial_value = lax.optimization_barrier(partial_value)
        return total + partial_value.astype(jnp.float32)
    total = lax.fori_loop(0, N_HEAD, add_group, jnp.zeros((length, D), jnp.float32))
    return total.astype(jnp.bfloat16)
```

```python
import functools

import jax
import jax.numpy as jnp
from jax import lax
from jax.experimental import pallas as pl
from jax.experimental.pallas import tpu as pltpu
from jax.sharding import PartitionSpec as P

MESH = pl.DeviceIdType.MESH
BF = jnp.bfloat16
F32 = jnp.float32
NZ = 16
CHIPS = 16
YS = 4
XS = 4
ROWS = 128
FEAT = 256
DK = 128
LAG = 6


def tree_step2():
    parent = {}
    for s in (1, -1):
        parent.update({2 * s: 0, 4 * s: 2 * s, 6 * s: 4 * s, s: 0, 3 * s: 2 * s, 5 * s: 4 * s, 7 * s: 6 * s})
    parent[8] = 6
    return [2, -2, 1, -1, 4, -4, 3, -3, 6, -6, 5, -5, 8, 7, -7], parent


def tree_step3():
    parent = {3: 0, -3: 0, 6: 3, -6: -3, 8: 6}
    for s in (0, 3, -3, 6, -6):
        parent[s + 1] = s
        parent[s - 1] = s
    return [3, -3, 1, -1, 6, -6, 4, -4, 2, -2, 5, -5, 7, -7, 8], parent


TREE_A = tree_step2()
TREE_D = tree_step3()


def split(a):
    high = a.astype(BF)
    return high, (a - high.astype(F32)).astype(BF)


def dot(a, b):
    return jnp.dot(a, b, preferred_element_type=F32)


def dot_nt(a, b):
    return lax.dot_general(a, b, (((1,), (1,)), ((), ())), preferred_element_type=F32)


def dot_tn(a, b):
    return lax.dot_general(a, b, (((0,), (0,)), ((), ())), preferred_element_type=F32)


def three(product, a, b):
    ah, al = a
    bh, bl = b
    return product(ah, bh) + (product(ah, bl) + product(al, bh))


def mm3(a, b):
    return three(dot, split(a), split(b))


def mm2(n, s):
    high, low = split(s)
    return dot(n, high) + dot(n, low)


def lower_inverse(low):
    r = lax.broadcasted_iota(jnp.int32, (ROWS, ROWS), 0)
    c = lax.broadcasted_iota(jnp.int32, (ROWS, ROWS), 1)
    b = 16
    count = ROWS // b
    diag = jnp.where((r // b) == (c // b), low, 0.0)
    x = (r == c).astype(F32).reshape(count, b, ROWS)
    for j in range(b - 1):
        col = jnp.sum(jnp.where((c % b) == j, diag, 0.0), axis=1, keepdims=True)
        x = x - col.reshape(count, b, 1) * x[:, j : j + 1, :]
    x = x.reshape(ROWS, ROWS)
    w = b
    while w < ROWS:
        off = jnp.where(((r // w) % 2 == 1) & ((c // w) == (r // w) - 1), low, 0.0)
        x = x - mm3(x, mm3(off, x))
        w *= 2
    return x


def kernel(
    tokens, w_query, w_key, w_value, w_beta, bias, w_out, out,
    own, tok, weights, wb32, acc, accb, wo, own_x, peer_x, total, chain, state, att_own, att,
    reader_s, local_s,
    load_sem, w_sem, a_send, a_recv, w1_send, w1_recv, w1_own, w2_send, w2_recv, w3_send, w3_recv,
    c_send, c_recv, p_send, p_recv, f_send, f_recv, d_send, d_recv, hello,
):
    z = lax.axis_index("head")
    ctx = lax.axis_index("ctx")
    core = lax.rem(ctx, 2)
    chip = ctx // 2
    x = chip // YS
    y = lax.rem(chip, YS)
    peer = ctx + 1 - 2 * core

    def head_at(off):
        return lax.rem(z + (off + 2 * NZ) % NZ, NZ)

    load = pltpu.make_async_copy(tokens, own, load_sem)
    load.start()
    w_loads = [
        pltpu.make_async_copy(w, weights.at[:, pl.ds(DK * i, DK)], w_sem.at[i])
        for i, w in enumerate((w_query, w_key, w_value))
    ]
    for w in w_loads:
        w.start()

    x_peers = [(lax.rem(x + d, XS) * YS + y) * 2 + core for d in (1, 2, 3)]
    y_peers = [(x * YS + lax.rem(y + d, YS)) * 2 + core for d in (1, 2, 3)]
    z_offs = sorted({(o - TREE_A[1][o]) % NZ for o in TREE_A[0]} | {(TREE_A[1][o] - o) % NZ for o in TREE_A[0]})
    barrier = pltpu.get_barrier_semaphore()
    for off in z_offs:
        pl.semaphore_signal(barrier, inc=1, device_id={"head": head_at(off)}, device_id_type=MESH)
    for c in x_peers + y_peers + [peer]:
        pl.semaphore_signal(barrier, inc=1, device_id={"ctx": c}, device_id_type=MESH)
    pl.semaphore_wait(barrier, len(z_offs) + 7)

    def tree_copies(order, parent, first, slots, send, recv):
        def copy(o):
            p = parent[o]
            return pltpu.make_async_remote_copy(
                src_ref=first if p == 0 else slots.at[p % NZ],
                dst_ref=slots.at[o % NZ],
                send_sem=send.at[o % NZ],
                recv_sem=recv.at[o % NZ],
                device_id={"head": head_at(o - p)},
                device_id_type=MESH,
            )

        kids = {}
        for o in order:
            kids.setdefault(parent[o], []).append(o)
        return copy, kids

    order_a, parent_a = TREE_A
    a_copy, a_kids = tree_copies(order_a, parent_a, own, tok, a_send, a_recv)
    load.wait()
    for o in a_kids[0]:
        a_copy(o).start()
    for c in x_peers:
        pl.semaphore_signal(hello, inc=1, device_id={"ctx": c}, device_id_type=MESH)

    row_tile = pl.multiple_of((chip // 2) * 16, 16)
    col_tile = pl.multiple_of(lax.rem(chip, 2) * 128, 128)
    half = lax.rem(core + z, 2)

    def tile_of(parity, index):
        return wo.at[parity, index, pl.ds(row_tile, 16), pl.ds(col_tile, 128)]

    def w1_copy(off):
        target = head_at(-off)
        return pltpu.make_async_remote_copy(
            src_ref=w_out.at[
                pl.ds(row_tile, 16), pl.ds(pl.multiple_of(target * FEAT + col_tile, 128), 128)
            ],
            dst_ref=tile_of(lax.rem(z, 2), z // 2),
            send_sem=w1_send.at[off % NZ],
            recv_sem=w1_recv.at[(-off) % NZ],
            device_id={"head": target},
            device_id_type=MESH,
        )

    w1_mine = pltpu.make_async_copy(
        w_out.at[pl.ds(row_tile, 16), pl.ds(pl.multiple_of(z * FEAT + col_tile, 128), 128)],
        tile_of(lax.rem(z, 2), z // 2),
        w1_own,
    )

    @pl.when(core == 0)
    def _():
        w1_mine.start()

    for w in w_loads:
        w.wait()
    for i in range(NZ):
        wb32[i : i + 1, :] = w_beta[:, i * FEAT : (i + 1) * FEAT].astype(F32)

    def project(block, off, first):
        owner = head_at(-off)
        rows = pl.ds(pl.multiple_of(owner * FEAT, FEAT), FEAT)
        part = dot(block, weights[rows, :])
        beta = block.astype(F32) * wb32[pl.ds(owner, 1), :]
        if first:
            acc[...] = part
            accb[...] = beta
        else:
            acc[...] += part
            accb[...] += beta

    project(own[...], 0, True)
    for o in order_a:
        a_copy(o).wait_recv()
        for q in a_kids.get(o, ()):
            a_copy(q).start()

        @pl.when(core == o % 2)
        def _():
            w1_copy(o).start()

        project(tok[o % NZ], o, False)

    def unit(m):
        return m / jnp.sqrt(jnp.sum(m * m, axis=1, keepdims=True) + 1e-06)

    query = unit(acc[:, 0:DK])
    key = unit(acc[:, DK : 2 * DK])
    value = acc[:, 2 * DK : 3 * DK]
    beta = jax.nn.sigmoid(jnp.sum(accb[...], axis=1, keepdims=True) + bias[0])
    r = lax.broadcasted_iota(jnp.int32, (ROWS, ROWS), 0)
    c = lax.broadcasted_iota(jnp.int32, (ROWS, ROWS), 1)
    key2 = split(key)
    inner = three(dot_nt, key2, key2)
    inverse = lower_inverse(jnp.where(r > c, beta * inner, 0.0))
    solved = mm3(inverse, jnp.concatenate([beta * key, beta * value], axis=1))
    solved2 = split(solved)
    mine = three(dot_tn, key2, solved2)
    own_x[...] = mine.astype(BF)
    c_copy = pltpu.make_async_remote_copy(
        src_ref=own_x, dst_ref=peer_x, send_sem=c_send, recv_sem=c_recv,
        device_id={"ctx": peer}, device_id_type=MESH,
    )
    c_copy.start()
    causal = jnp.where(r >= c, three(dot_nt, split(query), key2), 0.0)
    seen = three(dot, split(causal), solved2)
    reader_s[...] = query - seen[:, 0:DK]
    local_s[...] = seen[:, DK:]
    c_copy.wait_recv()
    other = peer_x[...].astype(F32)
    early = jnp.where(core == 0, mine, other)
    late = jnp.where(core == 0, other, mine)
    total[...] = (early + late - mm3(late[:, 0:DK], early)).astype(BF)

    mine_rows = pl.ds(pl.multiple_of(core * 64, 64), 64)
    pl.semaphore_wait(hello, 3)

    def p_copy(target):
        return pltpu.make_async_remote_copy(
            src_ref=total.at[mine_rows], dst_ref=chain.at[chip, mine_rows],
            send_sem=p_send.at[target], recv_sem=p_recv.at[chip],
            device_id={"ctx": target * 2 + core}, device_id_type=MESH,
        )

    def p_arrival(source):
        return pltpu.make_async_remote_copy(
            src_ref=total.at[mine_rows], dst_ref=chain.at[source, mine_rows],
            send_sem=p_send.at[source], recv_sem=p_recv.at[source],
            device_id={"ctx": source * 2 + core}, device_id_type=MESH,
        )

    def f_copy(source):
        return pltpu.make_async_remote_copy(
            src_ref=chain.at[source, mine_rows], dst_ref=chain.at[source, mine_rows],
            send_sem=f_send.at[source], recv_sem=f_recv.at[source],
            device_id={"ctx": peer}, device_id_type=MESH,
        )

    @pl.loop(0, CHIPS - 1)
    def _(i):
        target = CHIPS - 1 - i

        @pl.when(target > chip)
        def _():
            p_copy(target).start()

    for o in range(NZ):

        @pl.when(core == o % 2)
        def _():
            if o == 0:
                w1_mine.wait()
            else:
                w1_copy(-o).wait_recv()

    def w2_copy(d):
        target = lax.rem(chip + d, CHIPS)
        tiles = wo.at[half, :, pl.ds(row_tile, 16), pl.ds(col_tile, 128)]
        return pltpu.make_async_remote_copy(
            src_ref=tiles, dst_ref=tiles,
            send_sem=w2_send.at[d], recv_sem=w2_recv.at[d],
            device_id={"ctx": target * 2 + core}, device_id_type=MESH,
        )

    @pl.loop(1, CHIPS)
    def _(d):
        w2_copy(d).start()

    state[...] = jnp.zeros_like(state)

    @pl.loop(0, CHIPS - 1 + LAG)
    def _(t):
        @pl.when(t < chip)
        def _():
            p_arrival(t).wait_recv()
            f_copy(t).start()

        @pl.when((t >= LAG) & (t - LAG < chip))
        def _():
            s = t - LAG
            f_copy(s).wait_recv()
            step = chain[s]
            state[...] += step[:, DK:].astype(F32) - mm2(step[:, 0:DK], state[...])

    entry = state[...]
    moved = entry + peer_x[:, DK:].astype(F32) - mm2(peer_x[:, 0:DK], entry)
    entry = jnp.where(core == 0, entry, moved)
    att_own[...] = (local_s[...] + mm3(reader_s[...], entry)).astype(BF)

    order_d, parent_d = TREE_D
    d_copy, d_kids = tree_copies(order_d, parent_d, att_own, att, d_send, d_recv)
    for o in d_kids[0]:
        d_copy(o).start()

    def w2_arrival(d):
        source = lax.rem(chip + CHIPS - d, CHIPS)
        tiles = wo.at[
            half, :,
            pl.ds(pl.multiple_of((source // 2) * 16, 16), 16),
            pl.ds(pl.multiple_of(lax.rem(source, 2) * 128, 128), 128),
        ]
        return pltpu.make_async_remote_copy(
            src_ref=tiles, dst_ref=tiles,
            send_sem=w2_send.at[d], recv_sem=w2_recv.at[d],
            device_id={"ctx": source * 2 + core}, device_id_type=MESH,
        )

    @pl.loop(1, CHIPS)
    def _(d):
        w2_arrival(d).wait_recv()

    w3_copy = pltpu.make_async_remote_copy(
        src_ref=wo.at[half], dst_ref=wo.at[half], send_sem=w3_send, recv_sem=w3_recv,
        device_id={"ctx": peer}, device_id_type=MESH,
    )
    w3_copy.start()
    w3_arrival = pltpu.make_async_remote_copy(
        src_ref=wo.at[1 - half], dst_ref=wo.at[1 - half], send_sem=w3_send, recv_sem=w3_recv,
        device_id={"ctx": peer}, device_id_type=MESH,
    )
    w3_arrival.wait_recv()

    def columns(off):
        owner = head_at(-off)
        return wo[lax.rem(owner, 2), owner // 2]

    result = dot(att_own[...], columns(0))
    for o in order_d:
        d_copy(o).wait_recv()
        for q in d_kids.get(o, ()):
            d_copy(q).start()
        result = result + dot(att[o % NZ], columns(o))
    out[...] = result.astype(BF)

    for o in order_a:
        a_copy(o).wait_send()

        @pl.when(core == o % 2)
        def _():
            w1_copy(o).wait_send()

    c_copy.wait_send()

    @pl.loop(0, CHIPS)
    def _(i):
        @pl.when(i > chip)
        def _():
            p_copy(i).wait_send()

        @pl.when(i < chip)
        def _():
            f_copy(i).wait_send()

        @pl.when(i > 0)
        def _():
            w2_copy(i).wait_send()

    w3_copy.wait_send()
    for o in order_d:
        d_copy(o).wait_send()


def shards(tokens, w_query, w_key, w_value, w_beta, beta_bias, w_out):
    hbm = pl.BlockSpec(memory_space=pltpu.HBM)
    vmem = pl.BlockSpec(memory_space=pltpu.VMEM)
    smem = pl.BlockSpec(memory_space=pltpu.SMEM)
    dma = pltpu.SemaphoreType.DMA
    return pl.pallas_call(
        kernel,
        out_shape=jax.ShapeDtypeStruct((ROWS, FEAT), BF),
        in_specs=[hbm, hbm, hbm, hbm, vmem, smem, hbm],
        out_specs=vmem,
        scratch_shapes=[
            pltpu.VMEM((ROWS, FEAT), BF),
            pltpu.VMEM((NZ, ROWS, FEAT), BF),
            pltpu.VMEM((NZ * FEAT, 3 * DK), BF),
            pltpu.VMEM((NZ, FEAT), F32),
            pltpu.VMEM((ROWS, 3 * DK), F32),
            pltpu.VMEM((ROWS, FEAT), F32),
            pltpu.VMEM((2, NZ // 2, ROWS, FEAT), BF),
            pltpu.VMEM((ROWS, 2 * DK), BF),
            pltpu.VMEM((ROWS, 2 * DK), BF),
            pltpu.VMEM((ROWS, 2 * DK), BF),
            pltpu.VMEM((CHIPS, ROWS, 2 * DK), BF),
            pltpu.VMEM((DK, DK), F32),
            pltpu.VMEM((ROWS, DK), BF),
            pltpu.VMEM((NZ, ROWS, DK), BF),
            pltpu.VMEM((ROWS, DK), F32),
            pltpu.VMEM((ROWS, DK), F32),
            dma, dma((3,)), dma((NZ,)), dma((NZ,)),
            dma((NZ,)), dma((NZ,)), dma, dma((CHIPS,)), dma((CHIPS,)), dma, dma,
            dma, dma, dma((CHIPS,)), dma((CHIPS,)), dma((CHIPS,)), dma((CHIPS,)),
            dma((NZ,)), dma((NZ,)), pltpu.SemaphoreType.REGULAR,
        ],
        compiler_params=pltpu.CompilerParams(
            collective_id=0, has_side_effects=True, vmem_limit_bytes=63 * 2**20
        ),
    )(tokens, w_query, w_key, w_value, w_beta.T, beta_bias, w_out)


def solution(mesh):
    in_specs = (
        P("ctx", "head"),
        P(None, "head"),
        P(None, "head"),
        P(None, "head"),
        P(None, "head"),
        P("head"),
        P("head", None),
    )
    return jax.shard_map(
        shards, mesh=mesh, in_specs=in_specs, out_specs=P("ctx", "head"), check_vma=False
    )
```

```python
import functools

import jax
import jax.numpy as jnp
from jax import lax
from jax.experimental import pallas as pl
from jax.experimental.pallas import tpu as pltpu
from jax.sharding import PartitionSpec as P

MESH = pl.DeviceIdType.MESH
BF = jnp.bfloat16
F32 = jnp.float32
NZ = 16
CHIPS = 16
YS = 4
XS = 4
ROWS = 128
FEAT = 256
DK = 128
LAG = 4
W1_AT = 1
W2_AT = 10


def tree_step2():
    parent = {}
    for s in (1, -1):
        parent.update({2 * s: 0, 4 * s: 2 * s, 6 * s: 4 * s, 8 * s: 6 * s})
        parent.update({s: 0, 3 * s: 2 * s, 5 * s: 4 * s, 7 * s: 6 * s})
    return [2, -2, 1, -1, 4, -4, 3, -3, 6, -6, 5, -5, 8, -8, 7, -7], parent


def tree_seed5():
    parent = {8: 5, -8: -5}
    for s in (0, 5, -5):
        if s:
            parent[s] = 0
        for e in (1, -1, 2, -2):
            parent[s + e] = s
    return [5, -5, 1, -1, 2, -2, 4, -4, 6, -6, 3, -3, 7, -7, 8, -8], parent


TREE_A = tree_step2()
TREE_D = tree_seed5()


def split(a):
    high = a.astype(BF)
    return high, (a - high.astype(F32)).astype(BF)


def dot(a, b):
    return jnp.dot(a, b, preferred_element_type=F32)


def dot_nt(a, b):
    return lax.dot_general(a, b, (((1,), (1,)), ((), ())), preferred_element_type=F32)


def dot_tn(a, b):
    return lax.dot_general(a, b, (((0,), (0,)), ((), ())), preferred_element_type=F32)


def three(product, a, b):
    ah, al = a
    bh, bl = b
    return product(ah, bh) + (product(ah, bl) + product(al, bh))


def mm3(a, b):
    return three(dot, split(a), split(b))


def mm2(n, s):
    high, low = split(s)
    return dot(n, high) + dot(n, low)


def lower_inverse(low):
    r = lax.broadcasted_iota(jnp.int32, (ROWS, ROWS), 0)
    c = lax.broadcasted_iota(jnp.int32, (ROWS, ROWS), 1)
    b = 16
    count = ROWS // b
    diag = jnp.where((r // b) == (c // b), low, 0.0)
    x = (r == c).astype(F32).reshape(count, b, ROWS)
    for j in range(b - 1):
        col = jnp.sum(jnp.where((c % b) == j, diag, 0.0), axis=1, keepdims=True)
        x = x - col.reshape(count, b, 1) * x[:, j : j + 1, :]
    x = x.reshape(ROWS, ROWS)
    w = b
    while w < ROWS:
        off = jnp.where(((r // w) % 2 == 1) & ((c // w) == (r // w) - 1), low, 0.0)
        x = x - mm3(x, mm3(off, x))
        w *= 2
    return x


def kernel(
    tokens, w_query, w_key, w_value, w_beta_in, bias_in, w_out, out,
    w_beta, bias, own, tok, weights, wb32, acc, accb, wo, own_x, peer_x, total, chain, state, att_own, att,
    reader_s, local_s,
    load_sem, w_sem, a_send, a_recv, w1_send, w1_recv, w1_own, w2_send, w2_recv, w3_send, w3_recv,
    c_send, c_recv, pf_send, p_recv, f_recv, d_send, d_recv, hello,
):
    z = lax.axis_index("head")
    ctx = lax.axis_index("ctx")
    core = lax.rem(ctx, 2)
    chip = ctx // 2
    x = chip // YS
    y = lax.rem(chip, YS)
    peer = ctx + 1 - 2 * core

    def head_at(off):
        return lax.rem(z + off % NZ, NZ)

    x_peers = [(lax.rem(x + d, XS) * YS + y) * 2 + core for d in (1, 2, 3)]
    y_peers = [(x * YS + lax.rem(y + d, YS)) * 2 + core for d in (1, 2, 3)]
    z_offs = sorted({(o - TREE_A[1][o]) % NZ for o in TREE_A[0]} | {(TREE_A[1][o] - o) % NZ for o in TREE_A[0]})
    barrier = pltpu.get_barrier_semaphore()
    for off in z_offs:
        pl.semaphore_signal(barrier, inc=1, device_id={"head": head_at(off)}, device_id_type=MESH)
    for c in x_peers + y_peers + [peer]:
        pl.semaphore_signal(barrier, inc=1, device_id={"ctx": c}, device_id_type=MESH)

    load = pltpu.make_async_copy(tokens, own, load_sem)
    load.start()
    for i, w in enumerate((w_query, w_key, w_value)):
        pltpu.make_async_copy(w, weights.at[:, pl.ds(DK * i, DK)], w_sem.at[0]).start()
    w_loads = [
        pltpu.make_async_copy(weights, weights, w_sem.at[0]),
        pltpu.make_async_copy(w_beta_in, w_beta, w_sem.at[1]),
        pltpu.make_async_copy(bias_in, bias, w_sem.at[2]),
    ]
    for w in w_loads[1:]:
        w.start()
    pl.semaphore_wait(barrier, len(z_offs) + 7)

    def tree_copies(tree, first, slots, send, recv):
        order, parent = tree

        def copy(o):
            p = parent[o]
            target = head_at(o - p)
            if o in (8, -8):
                rows = pl.ds(0 if o > 0 else ROWS // 2, ROWS // 2)
            else:
                rows = pl.ds(0, ROWS)
            return pltpu.make_async_remote_copy(
                src_ref=first.at[rows] if p == 0 else slots.at[p % NZ, rows],
                dst_ref=slots.at[o % NZ, rows],
                send_sem=send,
                recv_sem=recv.at[0 if o == -8 else o % NZ],
                device_id={"head": target},
                device_id_type=MESH,
            )

        kids = {}
        for o in order:
            kids.setdefault(parent[o], []).append(o)
        return order, copy, kids

    order_a, a_copy, a_kids = tree_copies(TREE_A, tokens, tok, a_send, a_recv)
    for o in a_kids[0]:
        a_copy(o).start()
    for c in x_peers:
        pl.semaphore_signal(hello.at[0], inc=1, device_id={"ctx": c}, device_id_type=MESH)
    for off in (2, -2):
        pl.semaphore_signal(hello.at[1], inc=1, device_id={"head": head_at(off)}, device_id_type=MESH)

    row_tile = pl.multiple_of((chip // 2) * 16, 16)
    col_tile = pl.multiple_of(lax.rem(chip, 2) * 128, 128)
    half = lax.rem(core + z, 2)

    def tile_of(parity, index):
        return wo.at[parity, index, pl.ds(row_tile, 16), pl.ds(col_tile, 128)]

    def w1_copy(off):
        target = head_at(-off)
        return pltpu.make_async_remote_copy(
            src_ref=w_out.at[
                pl.ds(row_tile, 16), pl.ds(pl.multiple_of(target * FEAT + col_tile, 128), 128)
            ],
            dst_ref=tile_of(lax.rem(z, 2), z // 2),
            send_sem=w1_send,
            recv_sem=w1_recv,
            device_id={"head": target},
            device_id_type=MESH,
        )

    w1_mine = pltpu.make_async_copy(
        w_out.at[pl.ds(row_tile, 16), pl.ds(pl.multiple_of(z * FEAT + col_tile, 128), 128)],
        tile_of(lax.rem(z, 2), z // 2),
        w1_own,
    )

    @pl.when(core == 0)
    def _():
        w1_mine.start()

    for w in w_loads:
        w.wait()
    for i in range(NZ):
        wb32[i : i + 1, :] = w_beta[:, i * FEAT : (i + 1) * FEAT].astype(F32)

    def project(block, off, first):
        owner = head_at(-off)
        rows = pl.ds(pl.multiple_of(owner * FEAT, FEAT), FEAT)
        part = dot(block, weights[rows, :])
        beta = block.astype(F32) * wb32[pl.ds(owner, 1), :]
        if first:
            acc[...] = part
            accb[...] = beta
        else:
            acc[...] += part
            accb[...] += beta

    def bytes_of(ref, send, recv):
        return pltpu.make_async_remote_copy(
            src_ref=ref, dst_ref=ref, send_sem=send, recv_sem=recv,
            device_id={"ctx": peer}, device_id_type=MESH,
        )

    w1_counts = (NZ // 2 - 1, NZ // 2)

    def w1_bytes(count):
        return bytes_of(wo.at[0, pl.ds(0, count), pl.ds(0, 16), pl.ds(0, 128)], w1_send, w1_recv)

    w2_bytes = bytes_of(weights.at[pl.ds(0, 640)], w2_send, w2_recv)

    def w2_copy(d):
        target = lax.rem(chip + d, CHIPS)
        tiles = wo.at[half, :, pl.ds(row_tile, 16), pl.ds(col_tile, 128)]
        return pltpu.make_async_remote_copy(
            src_ref=tiles, dst_ref=tiles, send_sem=w2_send, recv_sem=w2_recv,
            device_id={"ctx": target * 2 + core}, device_id_type=MESH,
        )

    load.wait()
    project(own[...], 0, True)
    pl.semaphore_wait(hello.at[1], 2)
    for off in (4, -4):
        pl.semaphore_signal(hello.at[2], inc=1, device_id={"head": head_at(off)}, device_id_type=MESH)
    for step, o in enumerate(order_a):
        a_copy(o).wait_recv()
        for q in a_kids.get(o, ()):
            a_copy(q).start()
        if step == W1_AT:
            pl.semaphore_wait(hello.at[2], 2)
            for q in range(1, NZ):

                @pl.when(core == q % 2)
                def _():
                    w1_copy(q).start()

        if step == W2_AT:
            pl.semaphore_wait(hello.at[0], 3)
            for k in range(2):

                @pl.when(core == k)
                def _():
                    w1_bytes(w1_counts[k]).wait_recv()
                    if k == 0:
                        w1_mine.wait()

            @pl.loop(1, CHIPS)
            def _(d):
                w2_copy(d).start()

        if o != 8:
            project(tok[o % NZ], o, False)

    def unit(m):
        return m / jnp.sqrt(jnp.sum(m * m, axis=1, keepdims=True) + 1e-06)

    query = unit(acc[:, 0:DK])
    key = unit(acc[:, DK : 2 * DK])
    value = acc[:, 2 * DK : 3 * DK]
    beta = jax.nn.sigmoid(jnp.sum(accb[...], axis=1, keepdims=True) + bias[0])
    r = lax.broadcasted_iota(jnp.int32, (ROWS, ROWS), 0)
    c = lax.broadcasted_iota(jnp.int32, (ROWS, ROWS), 1)
    key2 = split(key)
    inner = three(dot_nt, key2, key2)
    inverse = lower_inverse(jnp.where(r > c, beta * inner, 0.0))
    solved = mm3(inverse, jnp.concatenate([beta * key, beta * value], axis=1))
    solved2 = split(solved)
    mine = three(dot_tn, key2, solved2)
    own_x[...] = mine.astype(BF)
    c_copy = pltpu.make_async_remote_copy(
        src_ref=own_x, dst_ref=peer_x, send_sem=c_send, recv_sem=c_recv,
        device_id={"ctx": peer}, device_id_type=MESH,
    )
    c_copy.start()
    causal = jnp.where(r >= c, three(dot_nt, split(query), key2), 0.0)
    seen = three(dot, split(causal), solved2)
    reader_s[...] = query - seen[:, 0:DK]
    local_s[...] = seen[:, DK:]
    c_copy.wait_recv()
    other = peer_x[...].astype(F32)
    early = jnp.where(core == 0, mine, other)
    late = jnp.where(core == 0, other, mine)
    total[...] = (early + late - mm2(late[:, 0:DK].astype(BF), early)).astype(BF)

    mine_rows = pl.ds(pl.multiple_of(core * 64, 64), 64)

    def p_copy(target):
        return pltpu.make_async_remote_copy(
            src_ref=total.at[mine_rows], dst_ref=chain.at[chip, mine_rows],
            send_sem=pf_send.at[target], recv_sem=p_recv.at[chip],
            device_id={"ctx": target * 2 + core}, device_id_type=MESH,
        )

    def p_arrival(source):
        return pltpu.make_async_remote_copy(
            src_ref=total.at[mine_rows], dst_ref=chain.at[source, mine_rows],
            send_sem=pf_send.at[source], recv_sem=p_recv.at[source],
            device_id={"ctx": source * 2 + core}, device_id_type=MESH,
        )

    def f_copy(source):
        return pltpu.make_async_remote_copy(
            src_ref=chain.at[source, mine_rows], dst_ref=chain.at[source, mine_rows],
            send_sem=pf_send.at[source], recv_sem=f_recv.at[source],
            device_id={"ctx": peer}, device_id_type=MESH,
        )

    @pl.loop(0, CHIPS - 1)
    def _(i):
        target = CHIPS - 1 - i

        @pl.when(target > chip)
        def _():
            p_copy(target).start()

    state[...] = jnp.zeros_like(state)

    @pl.loop(0, CHIPS - 1 + LAG)
    def _(t):
        @pl.when(t < chip)
        def _():
            p_arrival(t).wait_recv()
            f_copy(t).start()

        @pl.when((t >= LAG) & (t - LAG < chip))
        def _():
            s = t - LAG
            f_copy(s).wait_recv()
            step = chain[s]
            state[...] += step[:, DK:].astype(F32) - mm2(step[:, 0:DK], state[...])

    entry = state[...]
    moved = entry + peer_x[:, DK:].astype(F32) - mm2(peer_x[:, 0:DK], entry)
    entry = jnp.where(core == 0, entry, moved)
    att_own[...] = (local_s[...] + mm3(reader_s[...], entry)).astype(BF)

    order_d, d_copy, d_kids = tree_copies(TREE_D, att_own, att, d_send, d_recv)
    for o in d_kids[0]:
        d_copy(o).start()

    w2_bytes.wait_recv()
    w3_copy = pltpu.make_async_remote_copy(
        src_ref=wo.at[half], dst_ref=wo.at[half], send_sem=w3_send, recv_sem=w3_recv,
        device_id={"ctx": peer}, device_id_type=MESH,
    )
    w3_copy.start()
    w3_arrival = pltpu.make_async_remote_copy(
        src_ref=wo.at[1 - half], dst_ref=wo.at[1 - half], send_sem=w3_send, recv_sem=w3_recv,
        device_id={"ctx": peer}, device_id_type=MESH,
    )
    w3_arrival.wait_recv()

    def columns(off):
        owner = head_at(-off)
        return wo[lax.rem(owner, 2), owner // 2]

    result = dot(att_own[...], columns(0))
    for o in order_d:
        d_copy(o).wait_recv()
        for q in d_kids.get(o, ()):
            d_copy(q).start()
        if o != 8:
            result = result + dot(att[o % NZ], columns(o))
    out[...] = result.astype(BF)

    bytes_of(tok.at[pl.ds(0, NZ - 1)], a_send, a_send).wait_send()
    for k in range(2):

        @pl.when(core == k)
        def _():
            w1_bytes(w1_counts[k]).wait_send()

    w2_bytes.wait_send()
    c_copy.wait_send()

    @pl.loop(0, CHIPS)
    def _(i):
        @pl.when(i > chip)
        def _():
            p_copy(i).wait_send()

        @pl.when(i < chip)
        def _():
            f_copy(i).wait_send()

    w3_copy.wait_send()
    bytes_of(att.at[pl.ds(0, NZ - 1)], d_send, d_send).wait_send()


def shards(tokens, w_query, w_key, w_value, w_beta, beta_bias, w_out):
    hbm = pl.BlockSpec(memory_space=pltpu.HBM)
    vmem = pl.BlockSpec(memory_space=pltpu.VMEM)
    dma = pltpu.SemaphoreType.DMA
    return pl.pallas_call(
        kernel,
        out_shape=jax.ShapeDtypeStruct((ROWS, FEAT), BF),
        in_specs=[hbm] * 7,
        out_specs=vmem,
        scratch_shapes=[
            pltpu.VMEM((1, NZ * FEAT), BF),
            pltpu.SMEM((1,), F32),
            pltpu.VMEM((ROWS, FEAT), BF),
            pltpu.VMEM((NZ, ROWS, FEAT), BF),
            pltpu.VMEM((NZ * FEAT, 3 * DK), BF),
            pltpu.VMEM((NZ, FEAT), F32),
            pltpu.VMEM((ROWS, 3 * DK), F32),
            pltpu.VMEM((ROWS, FEAT), F32),
            pltpu.VMEM((2, NZ // 2, ROWS, FEAT), BF),
            pltpu.VMEM((ROWS, 2 * DK), BF),
            pltpu.VMEM((ROWS, 2 * DK), BF),
            pltpu.VMEM((ROWS, 2 * DK), BF),
            pltpu.VMEM((CHIPS, ROWS, 2 * DK), BF),
            pltpu.VMEM((DK, DK), F32),
            pltpu.VMEM((ROWS, DK), BF),
            pltpu.VMEM((NZ, ROWS, DK), BF),
            pltpu.VMEM((ROWS, DK), F32),
            pltpu.VMEM((ROWS, DK), F32),
            dma, dma((3,)), dma, dma((NZ,)), dma, dma, dma, dma, dma, dma, dma,
            dma, dma, dma((CHIPS,)), dma((CHIPS,)), dma((CHIPS,)), dma, dma((NZ,)),
            pltpu.SemaphoreType.REGULAR((3,)),
        ],
        compiler_params=pltpu.CompilerParams(
            collective_id=0, has_side_effects=True, vmem_limit_bytes=63 * 2**20
        ),
    )(tokens, w_query, w_key, w_value, w_beta.T, beta_bias, w_out)


def solution(mesh):
    in_specs = (
        P("ctx", "head"),
        P(None, "head"),
        P(None, "head"),
        P(None, "head"),
        P(None, "head"),
        P("head"),
        P("head", None),
    )
    return jax.shard_map(
        shards, mesh=mesh, in_specs=in_specs, out_specs=P("ctx", "head"), check_vma=False
    )
```

```python
import functools

import jax
import jax.numpy as jnp
from jax import lax
from jax.experimental import pallas as pl
from jax.experimental.pallas import tpu as pltpu
from jax.sharding import PartitionSpec as P

MESH = pl.DeviceIdType.MESH
BF = jnp.bfloat16
F32 = jnp.float32
NZ = 16
CHIPS = 16
YS = 4
XS = 4
ROWS = 128
FEAT = 256
DK = 128
LAG = 8
W1_AT = 1
W2_AT = 10


def tree_step2():
    parent = {}
    for s in (1, -1):
        parent.update({2 * s: 0, 4 * s: 2 * s, 6 * s: 4 * s, 8 * s: 6 * s})
        parent.update({s: 0, 3 * s: 2 * s, 5 * s: 4 * s, 7 * s: 6 * s})
    return [2, -2, 1, -1, 4, -4, 3, -3, 6, -6, 5, -5, 8, -8, 7, -7], parent


def tree_seed5():
    parent = {8: 5, -8: -5}
    for s in (0, 5, -5):
        if s:
            parent[s] = 0
        for e in (1, -1, 2, -2):
            parent[s + e] = s
    return [5, -5, 1, -1, 2, -2, 4, -4, 6, -6, 3, -3, 7, -7, 8, -8], parent


TREE_A = tree_step2()
TREE_D = tree_seed5()


def split(a):
    high = a.astype(BF)
    return high, (a - high.astype(F32)).astype(BF)


def dot(a, b):
    return jnp.dot(a, b, preferred_element_type=F32)


def dot_nt(a, b):
    return lax.dot_general(a, b, (((1,), (1,)), ((), ())), preferred_element_type=F32)


def dot_tn(a, b):
    return lax.dot_general(a, b, (((0,), (0,)), ((), ())), preferred_element_type=F32)


def three(product, a, b):
    ah, al = a
    bh, bl = b
    return product(ah, bh) + (product(ah, bl) + product(al, bh))


def mm3(a, b):
    return three(dot, split(a), split(b))


def mm2(n, s):
    high, low = split(s)
    return dot(n, high) + dot(n, low)


def lower_inverse(low):
    r = lax.broadcasted_iota(jnp.int32, (ROWS, ROWS), 0)
    c = lax.broadcasted_iota(jnp.int32, (ROWS, ROWS), 1)
    b = 16
    count = ROWS // b
    diag = jnp.where((r // b) == (c // b), low, 0.0)
    x = (r == c).astype(F32).reshape(count, b, ROWS)
    for j in range(b - 1):
        col = jnp.sum(jnp.where((c % b) == j, diag, 0.0), axis=1, keepdims=True)
        x = x - col.reshape(count, b, 1) * x[:, j : j + 1, :]
    x = x.reshape(ROWS, ROWS)
    w = b
    while w < ROWS:
        off = jnp.where(((r // w) % 2 == 1) & ((c // w) == (r // w) - 1), low, 0.0)
        x = x - mm3(x, mm3(off, x))
        w *= 2
    return x


def kernel(
    tokens, w_query, w_key, w_value, w_beta_in, bias_in, w_out, out,
    w_beta, bias, own, tok, weights, wb32, acc, accb, wo, own_x, peer_x, total, chain, state, att_own, att,
    reader_s, local_s,
    load_sem, w_sem, a_send, a_recv, w1_send, w1_recv, w1_own, w2_send, w2_recv, w3_send, w3_recv,
    c_send, c_recv, pf_send, p_recv, f_recv, d_send, d_recv, hello,
):
    z = lax.axis_index("head")
    ctx = lax.axis_index("ctx")
    core = lax.rem(ctx, 2)
    chip = ctx // 2
    x = chip // YS
    y = lax.rem(chip, YS)
    peer = ctx + 1 - 2 * core

    def head_at(off):
        return lax.rem(z + off % NZ, NZ)

    x_peers = [(lax.rem(x + d, XS) * YS + y) * 2 + core for d in (1, 2, 3)]
    y_peers = [(x * YS + lax.rem(y + d, YS)) * 2 + core for d in (1, 2, 3)]
    z_offs = sorted({(o - TREE_A[1][o]) % NZ for o in TREE_A[0]} | {(TREE_A[1][o] - o) % NZ for o in TREE_A[0]})
    barrier = pltpu.get_barrier_semaphore()
    for off in z_offs:
        pl.semaphore_signal(barrier, inc=1, device_id={"head": head_at(off)}, device_id_type=MESH)
    for c in x_peers + y_peers + [peer]:
        pl.semaphore_signal(barrier, inc=1, device_id={"ctx": c}, device_id_type=MESH)

    load = pltpu.make_async_copy(tokens, own, load_sem)
    load.start()
    for i, w in enumerate((w_query, w_key, w_value)):
        pltpu.make_async_copy(w, weights.at[:, pl.ds(DK * i, DK)], w_sem.at[0]).start()
    w_loads = [
        pltpu.make_async_copy(weights, weights, w_sem.at[0]),
        pltpu.make_async_copy(w_beta_in, w_beta, w_sem.at[1]),
        pltpu.make_async_copy(bias_in, bias, w_sem.at[2]),
    ]
    for w in w_loads[1:]:
        w.start()
    pl.semaphore_wait(barrier, len(z_offs) + 7)

    def tree_copies(tree, first, slots, send, recv):
        order, parent = tree

        def copy(o):
            p = parent[o]
            target = head_at(o - p)
            if o in (8, -8):
                rows = pl.ds(0 if o > 0 else ROWS // 2, ROWS // 2)
            else:
                rows = pl.ds(0, ROWS)
            return pltpu.make_async_remote_copy(
                src_ref=first.at[rows] if p == 0 else slots.at[p % NZ, rows],
                dst_ref=slots.at[o % NZ, rows],
                send_sem=send,
                recv_sem=recv.at[0 if o == -8 else o % NZ],
                device_id={"head": target},
                device_id_type=MESH,
            )

        kids = {}
        for o in order:
            kids.setdefault(parent[o], []).append(o)
        return order, copy, kids

    order_a, a_copy, a_kids = tree_copies(TREE_A, tokens, tok, a_send, a_recv)
    for o in a_kids[0]:
        a_copy(o).start()
    for c in x_peers:
        pl.semaphore_signal(hello.at[0], inc=1, device_id={"ctx": c}, device_id_type=MESH)
    for off in (2, -2):
        pl.semaphore_signal(hello.at[1], inc=1, device_id={"head": head_at(off)}, device_id_type=MESH)

    row_tile = pl.multiple_of((chip // 2) * 16, 16)
    col_tile = pl.multiple_of(lax.rem(chip, 2) * 128, 128)
    half = lax.rem(core + z, 2)

    def tile_of(parity, index):
        return wo.at[parity, index, pl.ds(row_tile, 16), pl.ds(col_tile, 128)]

    def w1_copy(off):
        target = head_at(-off)
        return pltpu.make_async_remote_copy(
            src_ref=w_out.at[
                pl.ds(row_tile, 16), pl.ds(pl.multiple_of(target * FEAT + col_tile, 128), 128)
            ],
            dst_ref=tile_of(lax.rem(z, 2), z // 2),
            send_sem=w1_send,
            recv_sem=w1_recv,
            device_id={"head": target},
            device_id_type=MESH,
        )

    w1_mine = pltpu.make_async_copy(
        w_out.at[pl.ds(row_tile, 16), pl.ds(pl.multiple_of(z * FEAT + col_tile, 128), 128)],
        tile_of(lax.rem(z, 2), z // 2),
        w1_own,
    )

    @pl.when(core == 0)
    def _():
        w1_mine.start()

    for w in w_loads:
        w.wait()
    for i in range(NZ):
        wb32[i : i + 1, :] = w_beta[:, i * FEAT : (i + 1) * FEAT].astype(F32)

    def project(block, off, first):
        owner = head_at(-off)
        rows = pl.ds(pl.multiple_of(owner * FEAT, FEAT), FEAT)
        part = dot(block, weights[rows, :])
        beta = block.astype(F32) * wb32[pl.ds(owner, 1), :]
        if first:
            acc[...] = part
            accb[...] = beta
        else:
            acc[...] += part
            accb[...] += beta

    def bytes_of(ref, send, recv):
        return pltpu.make_async_remote_copy(
            src_ref=ref, dst_ref=ref, send_sem=send, recv_sem=recv,
            device_id={"ctx": peer}, device_id_type=MESH,
        )

    w1_counts = (NZ // 2 - 1, NZ // 2)

    def w1_bytes(count):
        return bytes_of(wo.at[0, pl.ds(0, count), pl.ds(0, 16), pl.ds(0, 128)], w1_send, w1_recv)

    w2_bytes = bytes_of(weights.at[pl.ds(0, 640)], w2_send, w2_recv)

    def w2_copy(d):
        target = lax.rem(chip + d, CHIPS)
        tiles = wo.at[half, :, pl.ds(row_tile, 16), pl.ds(col_tile, 128)]
        return pltpu.make_async_remote_copy(
            src_ref=tiles, dst_ref=tiles, send_sem=w2_send, recv_sem=w2_recv,
            device_id={"ctx": target * 2 + core}, device_id_type=MESH,
        )

    load.wait()
    project(own[...], 0, True)
    pl.semaphore_wait(hello.at[1], 2)
    for off in (4, -4):
        pl.semaphore_signal(hello.at[2], inc=1, device_id={"head": head_at(off)}, device_id_type=MESH)
    for step, o in enumerate(order_a):
        a_copy(o).wait_recv()
        for q in a_kids.get(o, ()):
            a_copy(q).start()
        if step == W1_AT:
            pl.semaphore_wait(hello.at[2], 2)
            for q in range(1, NZ):

                @pl.when(core == q % 2)
                def _():
                    w1_copy(q).start()

        if step == W2_AT:
            pl.semaphore_wait(hello.at[0], 3)
            for k in range(2):

                @pl.when(core == k)
                def _():
                    w1_bytes(w1_counts[k]).wait_recv()
                    if k == 0:
                        w1_mine.wait()

            @pl.loop(1, CHIPS)
            def _(d):
                w2_copy(d).start()

        if o != 8:
            project(tok[o % NZ], o, False)

    def unit(m):
        return m / jnp.sqrt(jnp.sum(m * m, axis=1, keepdims=True) + 1e-06)

    query = unit(acc[:, 0:DK])
    key = unit(acc[:, DK : 2 * DK])
    value = acc[:, 2 * DK : 3 * DK]
    beta = jax.nn.sigmoid(jnp.sum(accb[...], axis=1, keepdims=True) + bias[0])
    r = lax.broadcasted_iota(jnp.int32, (ROWS, ROWS), 0)
    c = lax.broadcasted_iota(jnp.int32, (ROWS, ROWS), 1)
    key2 = split(key)
    inner = three(dot_nt, key2, key2)
    inverse = lower_inverse(jnp.where(r > c, beta * inner, 0.0))
    solved = mm3(inverse, jnp.concatenate([beta * key, beta * value], axis=1))
    solved2 = split(solved)
    mine = three(dot_tn, key2, solved2)
    own_x[...] = mine.astype(BF)
    c_copy = pltpu.make_async_remote_copy(
        src_ref=own_x, dst_ref=peer_x, send_sem=c_send, recv_sem=c_recv,
        device_id={"ctx": peer}, device_id_type=MESH,
    )
    c_copy.start()
    causal = jnp.where(r >= c, three(dot_nt, split(query), key2), 0.0)
    seen = three(dot, split(causal), solved2)
    reader_s[...] = query - seen[:, 0:DK]
    local_s[...] = seen[:, DK:]
    c_copy.wait_recv()
    other = peer_x[...].astype(F32)
    early = jnp.where(core == 0, mine, other)
    late = jnp.where(core == 0, other, mine)
    total[...] = (early + late - mm2(late[:, 0:DK].astype(BF), early)).astype(BF)

    mine_rows = pl.ds(pl.multiple_of(core * 64, 64), 64)

    def p_copy(target):
        return pltpu.make_async_remote_copy(
            src_ref=total.at[mine_rows], dst_ref=chain.at[chip, mine_rows],
            send_sem=pf_send.at[0], recv_sem=p_recv.at[chip],
            device_id={"ctx": target * 2 + core}, device_id_type=MESH,
        )

    def p_arrival(source):
        return pltpu.make_async_remote_copy(
            src_ref=total.at[mine_rows], dst_ref=chain.at[source, mine_rows],
            send_sem=pf_send.at[0], recv_sem=p_recv.at[source],
            device_id={"ctx": source * 2 + core}, device_id_type=MESH,
        )

    def f_copy(source):
        return pltpu.make_async_remote_copy(
            src_ref=chain.at[source, mine_rows], dst_ref=chain.at[source, mine_rows],
            send_sem=pf_send.at[1], recv_sem=f_recv.at[source],
            device_id={"ctx": peer}, device_id_type=MESH,
        )

    @pl.loop(0, CHIPS)
    def _(i):
        target = (XS - 1 - i // YS) * YS + lax.rem(y + 6 - lax.rem(i, YS), YS)

        @pl.when(target > chip)
        def _():
            p_copy(target).start()

    state[...] = jnp.zeros_like(state)

    @pl.loop(0, CHIPS - 1 + LAG)
    def _(t):
        @pl.when(t < chip)
        def _():
            p_arrival(t).wait_recv()
            f_copy(t).start()

        @pl.when((t >= LAG) & (t - LAG < chip))
        def _():
            s = t - LAG
            f_copy(s).wait_recv()
            step = chain[s]
            state[...] += step[:, DK:].astype(F32) - mm2(step[:, 0:DK], state[...])

    entry = state[...]
    moved = entry + peer_x[:, DK:].astype(F32) - mm2(peer_x[:, 0:DK], entry)
    entry = jnp.where(core == 0, entry, moved)
    att_own[...] = (local_s[...] + mm3(reader_s[...], entry)).astype(BF)

    order_d, d_copy, d_kids = tree_copies(TREE_D, att_own, att, d_send, d_recv)
    for o in d_kids[0]:
        d_copy(o).start()

    w2_bytes.wait_recv()
    w3_copy = pltpu.make_async_remote_copy(
        src_ref=wo.at[half], dst_ref=wo.at[half], send_sem=w3_send, recv_sem=w3_recv,
        device_id={"ctx": peer}, device_id_type=MESH,
    )
    w3_copy.start()
    w3_arrival = pltpu.make_async_remote_copy(
        src_ref=wo.at[1 - half], dst_ref=wo.at[1 - half], send_sem=w3_send, recv_sem=w3_recv,
        device_id={"ctx": peer}, device_id_type=MESH,
    )
    w3_arrival.wait_recv()

    bytes_of(tok.at[pl.ds(0, NZ - 1)], a_send, a_send).wait_send()
    for k in range(2):

        @pl.when(core == k)
        def _():
            w1_bytes(w1_counts[k]).wait_send()

    w2_bytes.wait_send()
    c_copy.wait_send()

    def chain_bytes(count, send):
        return bytes_of(chain.at[pl.ds(0, count), pl.ds(0, ROWS // 2)], send, send)

    for i in range(CHIPS):

        @pl.when(chip == i)
        def _():
            if i < CHIPS - 1:
                chain_bytes(CHIPS - 1 - i, pf_send.at[0]).wait_send()
            if i > 0:
                chain_bytes(i, pf_send.at[1]).wait_send()


    def columns(off):
        owner = head_at(-off)
        return wo[lax.rem(owner, 2), owner // 2]

    result = dot(att_own[...], columns(0))
    for o in order_d:
        d_copy(o).wait_recv()
        for q in d_kids.get(o, ()):
            d_copy(q).start()
        if o != 8:
            result = result + dot(att[o % NZ], columns(o))
    out[...] = result.astype(BF)

    w3_copy.wait_send()
    bytes_of(att.at[pl.ds(0, NZ - 1)], d_send, d_send).wait_send()


def shards(tokens, w_query, w_key, w_value, w_beta, beta_bias, w_out):
    hbm = pl.BlockSpec(memory_space=pltpu.HBM)
    vmem = pl.BlockSpec(memory_space=pltpu.VMEM)
    dma = pltpu.SemaphoreType.DMA
    return pl.pallas_call(
        kernel,
        out_shape=jax.ShapeDtypeStruct((ROWS, FEAT), BF),
        in_specs=[hbm] * 7,
        out_specs=vmem,
        scratch_shapes=[
            pltpu.VMEM((1, NZ * FEAT), BF),
            pltpu.SMEM((1,), F32),
            pltpu.VMEM((ROWS, FEAT), BF),
            pltpu.VMEM((NZ, ROWS, FEAT), BF),
            pltpu.VMEM((NZ * FEAT, 3 * DK), BF),
            pltpu.VMEM((NZ, FEAT), F32),
            pltpu.VMEM((ROWS, 3 * DK), F32),
            pltpu.VMEM((ROWS, FEAT), F32),
            pltpu.VMEM((2, NZ // 2, ROWS, FEAT), BF),
            pltpu.VMEM((ROWS, 2 * DK), BF),
            pltpu.VMEM((ROWS, 2 * DK), BF),
            pltpu.VMEM((ROWS, 2 * DK), BF),
            pltpu.VMEM((CHIPS, ROWS, 2 * DK), BF),
            pltpu.VMEM((DK, DK), F32),
            pltpu.VMEM((ROWS, DK), BF),
            pltpu.VMEM((NZ, ROWS, DK), BF),
            pltpu.VMEM((ROWS, DK), F32),
            pltpu.VMEM((ROWS, DK), F32),
            dma, dma((3,)), dma, dma((NZ,)), dma, dma, dma, dma, dma, dma, dma,
            dma, dma, dma((2,)), dma((CHIPS,)), dma((CHIPS,)), dma, dma((NZ,)),
            pltpu.SemaphoreType.REGULAR((3,)),
        ],
        compiler_params=pltpu.CompilerParams(
            collective_id=0, has_side_effects=True, vmem_limit_bytes=63 * 2**20
        ),
    )(tokens, w_query, w_key, w_value, w_beta.T, beta_bias, w_out)


def solution(mesh):
    in_specs = (
        P("ctx", "head"),
        P(None, "head"),
        P(None, "head"),
        P(None, "head"),
        P(None, "head"),
        P("head"),
        P("head", None),
    )
    return jax.shard_map(
        shards, mesh=mesh, in_specs=in_specs, out_specs=P("ctx", "head"), check_vma=False
    )
```

```python
import functools

import jax
import jax.numpy as jnp
from jax import lax
from jax.experimental import pallas as pl
from jax.experimental.pallas import tpu as pltpu
from jax.sharding import PartitionSpec as P

MESH = pl.DeviceIdType.MESH
BF = jnp.bfloat16
F32 = jnp.float32
NZ = 16
CHIPS = 16
YS = 4
XS = 4
ROWS = 128
FEAT = 256
DK = 128
LAG = 8
W1_AT = 1
W2_AT = 10


def tree_step2():
    parent = {}
    for s in (1, -1):
        parent.update({2 * s: 0, 4 * s: 2 * s, 6 * s: 4 * s, 8 * s: 6 * s})
        parent.update({s: 0, 3 * s: 2 * s, 5 * s: 4 * s, 7 * s: 6 * s})
    return [2, -2, 1, -1, 4, -4, 3, -3, 6, -6, 5, -5, 8, -8, 7, -7], parent


def tree_seed5():
    parent = {8: 5, -8: -5}
    for s in (0, 5, -5):
        if s:
            parent[s] = 0
        for e in (1, -1, 2, -2):
            parent[s + e] = s
    parent.update({3: 2, -3: -2})
    return [5, -5, 2, -2, 1, -1, 3, -3, 7, -7, 4, -4, 6, -6, 8, -8], parent


TREE_A = tree_step2()
TREE_D = tree_seed5()


def split(a):
    high = a.astype(BF)
    return high, (a - high.astype(F32)).astype(BF)


def dot(a, b):
    return jnp.dot(a, b, preferred_element_type=F32)


def dot_nt(a, b):
    return lax.dot_general(a, b, (((1,), (1,)), ((), ())), preferred_element_type=F32)


def dot_tn(a, b):
    return lax.dot_general(a, b, (((0,), (0,)), ((), ())), preferred_element_type=F32)


def three(product, a, b):
    ah, al = a
    bh, bl = b
    return product(ah, bh) + (product(ah, bl) + product(al, bh))


def mm3(a, b):
    return three(dot, split(a), split(b))


def mm2(n, s):
    high, low = split(s)
    return dot(n, high) + dot(n, low)


def lower_inverse(low):
    r = lax.broadcasted_iota(jnp.int32, (ROWS, ROWS), 0)
    c = lax.broadcasted_iota(jnp.int32, (ROWS, ROWS), 1)
    b = 16
    count = ROWS // b
    diag = jnp.where((r // b) == (c // b), low, 0.0)
    x = (r == c).astype(F32).reshape(count, b, ROWS)
    for j in range(b - 1):
        col = jnp.sum(jnp.where((c % b) == j, diag, 0.0), axis=1, keepdims=True)
        x = x - col.reshape(count, b, 1) * x[:, j : j + 1, :]
    x = x.reshape(ROWS, ROWS)
    w = b
    while w < ROWS:
        off = jnp.where(((r // w) % 2 == 1) & ((c // w) == (r // w) - 1), low, 0.0)
        x = x - mm3(x, mm3(off, x))
        w *= 2
    return x


def kernel(
    tokens, w_query, w_key, w_value, w_beta_in, bias_in, w_out, out,
    w_beta, bias, own, tok, weights, wb32, acc, accb, wo, own_x, peer_x, total, chain, state, att_own, att,
    reader_s, local_s,
    load_sem, w_sem, a_send, a_recv, w1_send, w1_recv, w1_own, w2_send, w2_recv, w3_send, w3_recv,
    c_send, c_recv, pf_send, p_recv, f_recv, d_send, d_recv, hello,
):
    z = lax.axis_index("head")
    ctx = lax.axis_index("ctx")
    core = lax.rem(ctx, 2)
    chip = ctx // 2
    x = chip // YS
    y = lax.rem(chip, YS)
    peer = ctx + 1 - 2 * core

    def head_at(off):
        return lax.rem(z + off % NZ, NZ)

    x_peers = [(lax.rem(x + d, XS) * YS + y) * 2 + core for d in (1, 2, 3)]
    y_peers = [(x * YS + lax.rem(y + d, YS)) * 2 + core for d in (1, 2, 3)]
    z_offs = sorted({(o - TREE_A[1][o]) % NZ for o in TREE_A[0]} | {(TREE_A[1][o] - o) % NZ for o in TREE_A[0]})
    barrier = pltpu.get_barrier_semaphore()
    for off in z_offs:
        pl.semaphore_signal(barrier, inc=1, device_id={"head": head_at(off)}, device_id_type=MESH)
    for c in x_peers + y_peers + [peer]:
        pl.semaphore_signal(barrier, inc=1, device_id={"ctx": c}, device_id_type=MESH)

    load = pltpu.make_async_copy(tokens, own, load_sem)
    load.start()
    for i, w in enumerate((w_query, w_key, w_value)):
        pltpu.make_async_copy(w, weights.at[:, pl.ds(DK * i, DK)], w_sem.at[0]).start()
    w_loads = [
        pltpu.make_async_copy(weights, weights, w_sem.at[0]),
        pltpu.make_async_copy(w_beta_in, w_beta, w_sem.at[1]),
        pltpu.make_async_copy(bias_in, bias, w_sem.at[2]),
    ]
    for w in w_loads[1:]:
        w.start()
    pl.semaphore_wait(barrier, len(z_offs) + 7)

    def tree_copies(tree, first, slots, send, recv):
        order, parent = tree

        def copy(o):
            p = parent[o]
            target = head_at(o - p)
            if o in (8, -8):
                rows = pl.ds(0 if o > 0 else ROWS // 2, ROWS // 2)
            else:
                rows = pl.ds(0, ROWS)
            return pltpu.make_async_remote_copy(
                src_ref=first.at[rows] if p == 0 else slots.at[p % NZ, rows],
                dst_ref=slots.at[o % NZ, rows],
                send_sem=send,
                recv_sem=recv.at[0 if o == -8 else o % NZ],
                device_id={"head": target},
                device_id_type=MESH,
            )

        kids = {}
        for o in order:
            kids.setdefault(parent[o], []).append(o)
        return order, copy, kids

    order_a, a_copy, a_kids = tree_copies(TREE_A, tokens, tok, a_send, a_recv)
    for o in a_kids[0]:
        a_copy(o).start()
    for c in x_peers:
        pl.semaphore_signal(hello.at[0], inc=1, device_id={"ctx": c}, device_id_type=MESH)
    for off in (2, -2):
        pl.semaphore_signal(hello.at[1], inc=1, device_id={"head": head_at(off)}, device_id_type=MESH)

    row_tile = pl.multiple_of((chip // 2) * 16, 16)
    col_tile = pl.multiple_of(lax.rem(chip, 2) * 128, 128)
    half = lax.rem(core + z, 2)

    def tile_of(parity, index):
        return wo.at[parity, index, pl.ds(row_tile, 16), pl.ds(col_tile, 128)]

    def w1_copy(off):
        target = head_at(-off)
        return pltpu.make_async_remote_copy(
            src_ref=w_out.at[
                pl.ds(row_tile, 16), pl.ds(pl.multiple_of(target * FEAT + col_tile, 128), 128)
            ],
            dst_ref=tile_of(lax.rem(z, 2), z // 2),
            send_sem=w1_send,
            recv_sem=w1_recv,
            device_id={"head": target},
            device_id_type=MESH,
        )

    w1_mine = pltpu.make_async_copy(
        w_out.at[pl.ds(row_tile, 16), pl.ds(pl.multiple_of(z * FEAT + col_tile, 128), 128)],
        tile_of(lax.rem(z, 2), z // 2),
        w1_own,
    )

    @pl.when(core == 0)
    def _():
        w1_mine.start()

    for w in w_loads:
        w.wait()
    for i in range(NZ):
        wb32[i : i + 1, :] = w_beta[:, i * FEAT : (i + 1) * FEAT].astype(F32)

    def project(block, off, first):
        owner = head_at(-off)
        rows = pl.ds(pl.multiple_of(owner * FEAT, FEAT), FEAT)
        part = dot(block, weights[rows, :])
        beta = block.astype(F32) * wb32[pl.ds(owner, 1), :]
        if first:
            acc[...] = part
            accb[...] = beta
        else:
            acc[...] += part
            accb[...] += beta

    def bytes_of(ref, send, recv):
        return pltpu.make_async_remote_copy(
            src_ref=ref, dst_ref=ref, send_sem=send, recv_sem=recv,
            device_id={"ctx": peer}, device_id_type=MESH,
        )

    w1_counts = (NZ // 2 - 1, NZ // 2)

    def w1_bytes(count):
        return bytes_of(wo.at[0, pl.ds(0, count), pl.ds(0, 16), pl.ds(0, 128)], w1_send, w1_recv)

    w2_bytes = bytes_of(weights.at[pl.ds(0, 640)], w2_send, w2_recv)

    def w2_copy(d):
        target = lax.rem(chip + d, CHIPS)
        tiles = wo.at[half, :, pl.ds(row_tile, 16), pl.ds(col_tile, 128)]
        return pltpu.make_async_remote_copy(
            src_ref=tiles, dst_ref=tiles, send_sem=w2_send, recv_sem=w2_recv,
            device_id={"ctx": target * 2 + core}, device_id_type=MESH,
        )

    load.wait()
    project(own[...], 0, True)
    pl.semaphore_wait(hello.at[1], 2)
    for off in (4, -4):
        pl.semaphore_signal(hello.at[2], inc=1, device_id={"head": head_at(off)}, device_id_type=MESH)
    for step, o in enumerate(order_a):
        a_copy(o).wait_recv()
        for q in a_kids.get(o, ()):
            a_copy(q).start()
        if step == W1_AT:
            pl.semaphore_wait(hello.at[2], 2)
            for q in range(1, NZ):

                @pl.when(core == q % 2)
                def _():
                    w1_copy(q).start()

        if step == W2_AT:
            pl.semaphore_wait(hello.at[0], 3)
            for k in range(2):

                @pl.when(core == k)
                def _():
                    w1_bytes(w1_counts[k]).wait_recv()
                    if k == 0:
                        w1_mine.wait()

            @pl.loop(1, CHIPS)
            def _(d):
                w2_copy(d).start()

        if o != 8:
            project(tok[o % NZ], o, False)

    def unit(m):
        return m / jnp.sqrt(jnp.sum(m * m, axis=1, keepdims=True) + 1e-06)

    query = unit(acc[:, 0:DK])
    key = unit(acc[:, DK : 2 * DK])
    value = acc[:, 2 * DK : 3 * DK]
    beta = jax.nn.sigmoid(jnp.sum(accb[...], axis=1, keepdims=True) + bias[0])
    r = lax.broadcasted_iota(jnp.int32, (ROWS, ROWS), 0)
    c = lax.broadcasted_iota(jnp.int32, (ROWS, ROWS), 1)
    key2 = split(key)
    inner = three(dot_nt, key2, key2)
    inverse = lower_inverse(jnp.where(r > c, beta * inner, 0.0))
    solved = mm3(inverse, jnp.concatenate([beta * key, beta * value], axis=1))
    solved2 = split(solved)
    mine = three(dot_tn, key2, solved2)
    own_x[...] = mine.astype(BF)
    c_copy = pltpu.make_async_remote_copy(
        src_ref=own_x, dst_ref=peer_x, send_sem=c_send, recv_sem=c_recv,
        device_id={"ctx": peer}, device_id_type=MESH,
    )
    c_copy.start()
    causal = jnp.where(r >= c, three(dot_nt, split(query), key2), 0.0)
    seen = three(dot, split(causal), solved2)
    reader_s[...] = query - seen[:, 0:DK]
    local_s[...] = seen[:, DK:]
    c_copy.wait_recv()
    other = peer_x[...].astype(F32)
    early = jnp.where(core == 0, mine, other)
    late = jnp.where(core == 0, other, mine)
    total[...] = (early + late - mm2(late[:, 0:DK].astype(BF), early)).astype(BF)

    mine_rows = pl.ds(pl.multiple_of(core * 64, 64), 64)

    def p_copy(target):
        return pltpu.make_async_remote_copy(
            src_ref=total.at[mine_rows], dst_ref=chain.at[chip, mine_rows],
            send_sem=pf_send.at[0], recv_sem=p_recv.at[chip],
            device_id={"ctx": target * 2 + core}, device_id_type=MESH,
        )

    def p_arrival(source):
        return pltpu.make_async_remote_copy(
            src_ref=total.at[mine_rows], dst_ref=chain.at[source, mine_rows],
            send_sem=pf_send.at[0], recv_sem=p_recv.at[source],
            device_id={"ctx": source * 2 + core}, device_id_type=MESH,
        )

    def f_copy(source):
        return pltpu.make_async_remote_copy(
            src_ref=chain.at[source, mine_rows], dst_ref=chain.at[source, mine_rows],
            send_sem=pf_send.at[1], recv_sem=f_recv.at[source],
            device_id={"ctx": peer}, device_id_type=MESH,
        )

    @pl.loop(0, CHIPS)
    def _(i):
        target = (XS - 1 - i // YS) * YS + lax.rem(y + 6 - lax.rem(i, YS), YS)

        @pl.when(target > chip)
        def _():
            p_copy(target).start()

    state[...] = jnp.zeros_like(state)

    @pl.loop(0, CHIPS - 1 + LAG)
    def _(t):
        @pl.when(t < chip)
        def _():
            p_arrival(t).wait_recv()
            f_copy(t).start()

        @pl.when((t >= LAG) & (t - LAG < chip))
        def _():
            s = t - LAG
            f_copy(s).wait_recv()
            step = chain[s]
            state[...] += step[:, DK:].astype(F32) - mm2(step[:, 0:DK], state[...])

    entry = state[...]
    moved = entry + peer_x[:, DK:].astype(F32) - mm2(peer_x[:, 0:DK], entry)
    entry = jnp.where(core == 0, entry, moved)
    att_own[...] = (local_s[...] + mm3(reader_s[...], entry)).astype(BF)

    order_d, d_copy, d_kids = tree_copies(TREE_D, att_own, att, d_send, d_recv)
    for o in d_kids[0]:
        d_copy(o).start()

    w2_bytes.wait_recv()
    w3_copy = pltpu.make_async_remote_copy(
        src_ref=wo.at[half], dst_ref=wo.at[half], send_sem=w3_send, recv_sem=w3_recv,
        device_id={"ctx": peer}, device_id_type=MESH,
    )
    w3_copy.start()
    w3_arrival = pltpu.make_async_remote_copy(
        src_ref=wo.at[1 - half], dst_ref=wo.at[1 - half], send_sem=w3_send, recv_sem=w3_recv,
        device_id={"ctx": peer}, device_id_type=MESH,
    )
    w3_arrival.wait_recv()

    bytes_of(tok.at[pl.ds(0, NZ - 1)], a_send, a_send).wait_send()
    for k in range(2):

        @pl.when(core == k)
        def _():
            w1_bytes(w1_counts[k]).wait_send()

    w2_bytes.wait_send()
    c_copy.wait_send()

    def chain_bytes(count, send):
        return bytes_of(chain.at[pl.ds(0, count), pl.ds(0, ROWS // 2)], send, send)

    for i in range(CHIPS):

        @pl.when(chip == i)
        def _():
            if i < CHIPS - 1:
                chain_bytes(CHIPS - 1 - i, pf_send.at[0]).wait_send()
            if i > 0:
                chain_bytes(i, pf_send.at[1]).wait_send()


    def columns(off):
        owner = head_at(-off)
        return wo[lax.rem(owner, 2), owner // 2]

    result = dot(att_own[...], columns(0))
    for o in order_d:
        d_copy(o).wait_recv()
        for q in d_kids.get(o, ()):
            d_copy(q).start()
        if o != 8:
            result = result + dot(att[o % NZ], columns(o))
    out[...] = result.astype(BF)

    w3_copy.wait_send()
    bytes_of(att.at[pl.ds(0, NZ - 1)], d_send, d_send).wait_send()


def shards(tokens, w_query, w_key, w_value, w_beta, beta_bias, w_out):
    hbm = pl.BlockSpec(memory_space=pltpu.HBM)
    vmem = pl.BlockSpec(memory_space=pltpu.VMEM)
    dma = pltpu.SemaphoreType.DMA
    return pl.pallas_call(
        kernel,
        out_shape=jax.ShapeDtypeStruct((ROWS, FEAT), BF),
        in_specs=[hbm] * 7,
        out_specs=vmem,
        scratch_shapes=[
            pltpu.VMEM((1, NZ * FEAT), BF),
            pltpu.SMEM((1,), F32),
            pltpu.VMEM((ROWS, FEAT), BF),
            pltpu.VMEM((NZ, ROWS, FEAT), BF),
            pltpu.VMEM((NZ * FEAT, 3 * DK), BF),
            pltpu.VMEM((NZ, FEAT), F32),
            pltpu.VMEM((ROWS, 3 * DK), F32),
            pltpu.VMEM((ROWS, FEAT), F32),
            pltpu.VMEM((2, NZ // 2, ROWS, FEAT), BF),
            pltpu.VMEM((ROWS, 2 * DK), BF),
            pltpu.VMEM((ROWS, 2 * DK), BF),
            pltpu.VMEM((ROWS, 2 * DK), BF),
            pltpu.VMEM((CHIPS, ROWS, 2 * DK), BF),
            pltpu.VMEM((DK, DK), F32),
            pltpu.VMEM((ROWS, DK), BF),
            pltpu.VMEM((NZ, ROWS, DK), BF),
            pltpu.VMEM((ROWS, DK), F32),
            pltpu.VMEM((ROWS, DK), F32),
            dma, dma((3,)), dma, dma((NZ,)), dma, dma, dma, dma, dma, dma, dma,
            dma, dma, dma((2,)), dma((CHIPS,)), dma((CHIPS,)), dma, dma((NZ,)),
            pltpu.SemaphoreType.REGULAR((3,)),
        ],
        compiler_params=pltpu.CompilerParams(
            collective_id=0, has_side_effects=True, vmem_limit_bytes=63 * 2**20
        ),
    )(tokens, w_query, w_key, w_value, w_beta.T, beta_bias, w_out)


def solution(mesh):
    in_specs = (
        P("ctx", "head"),
        P(None, "head"),
        P(None, "head"),
        P(None, "head"),
        P(None, "head"),
        P("head"),
        P("head", None),
    )
    return jax.shard_map(
        shards, mesh=mesh, in_specs=in_specs, out_specs=P("ctx", "head"), check_vma=False
    )
```

```python
import functools

import jax
import jax.numpy as jnp
from jax import lax
from jax.experimental import pallas as pl
from jax.experimental.pallas import tpu as pltpu
from jax.sharding import PartitionSpec as P

MESH = pl.DeviceIdType.MESH
BF = jnp.bfloat16
F32 = jnp.float32
NZ = 16
CHIPS = 16
YS = 4
XS = 4
ROWS = 128
FEAT = 256
DK = 128
LAG = 8
W1_AT = 1
W2_AT = 12


def tree_step2():
    parent = {}
    for s in (1, -1):
        parent.update({2 * s: 0, 4 * s: 2 * s, 6 * s: 4 * s, 8 * s: 6 * s})
        parent.update({s: 0, 3 * s: 2 * s, 5 * s: 4 * s, 7 * s: 6 * s})
    return [2, -2, 4, -4, 1, -1, 6, -6, 3, -3, 8, -8, 5, -5, 7, -7], parent


def tree_seed5():
    parent = {8: 5, -8: -5}
    for s in (0, 5, -5):
        if s:
            parent[s] = 0
        for e in (1, -1, 2, -2):
            parent[s + e] = s
    parent.update({3: 2, -3: -2})
    return [5, -5, 2, -2, 1, -1, 3, -3, 7, -7, 4, -4, 6, -6, 8, -8], parent


TREE_A = tree_step2()
TREE_D = tree_seed5()


def split(a):
    high = a.astype(BF)
    return high, (a - high.astype(F32)).astype(BF)


def dot(a, b):
    return jnp.dot(a, b, preferred_element_type=F32)


def dot_nt(a, b):
    return lax.dot_general(a, b, (((1,), (1,)), ((), ())), preferred_element_type=F32)


def dot_tn(a, b):
    return lax.dot_general(a, b, (((0,), (0,)), ((), ())), preferred_element_type=F32)


def three(product, a, b):
    ah, al = a
    bh, bl = b
    return product(ah, bh) + (product(ah, bl) + product(al, bh))


def mm3(a, b):
    return three(dot, split(a), split(b))


def mm2(n, s):
    high, low = split(s)
    return dot(n, high) + dot(n, low)


def lower_inverse(low):
    r = lax.broadcasted_iota(jnp.int32, (ROWS, ROWS), 0)
    c = lax.broadcasted_iota(jnp.int32, (ROWS, ROWS), 1)
    b = 16
    count = ROWS // b
    diag = jnp.where((r // b) == (c // b), low, 0.0)
    x = (r == c).astype(F32).reshape(count, b, ROWS)
    for j in range(b - 1):
        col = jnp.sum(jnp.where((c % b) == j, diag, 0.0), axis=1, keepdims=True)
        x = x - col.reshape(count, b, 1) * x[:, j : j + 1, :]
    x = x.reshape(ROWS, ROWS)
    w = b
    while w < ROWS:
        off = jnp.where(((r // w) % 2 == 1) & ((c // w) == (r // w) - 1), low, 0.0)
        x = x - mm3(x, mm3(off, x))
        w *= 2
    return x


def kernel(
    tokens, w_query, w_key, w_value, w_beta_in, bias_in, w_out, out,
    w_beta, bias, own, tok, weights, wb32, acc, accb, wo, own_x, peer_x, total, chain, state, att_own, att,
    reader_s, local_s,
    load_sem, w_sem, a_send, a_recv, w1_send, w1_recv, w1_own, w2_send, w2_recv, w3_send, w3_recv,
    c_send, c_recv, pf_send, p_recv, f_recv, d_send, d_recv, hello,
):
    z = lax.axis_index("head")
    ctx = lax.axis_index("ctx")
    core = lax.rem(ctx, 2)
    chip = ctx // 2
    x = chip // YS
    y = lax.rem(chip, YS)
    peer = ctx + 1 - 2 * core

    def head_at(off):
        return lax.rem(z + off % NZ, NZ)

    x_peers = [(lax.rem(x + d, XS) * YS + y) * 2 + core for d in (1, 2, 3)]
    y_peers = [(x * YS + lax.rem(y + d, YS)) * 2 + core for d in (1, 2, 3)]
    z_offs = sorted({(o - TREE_A[1][o]) % NZ for o in TREE_A[0]} | {(TREE_A[1][o] - o) % NZ for o in TREE_A[0]})
    barrier = pltpu.get_barrier_semaphore()
    for off in z_offs:
        pl.semaphore_signal(barrier, inc=1, device_id={"head": head_at(off)}, device_id_type=MESH)
    for c in x_peers + y_peers + [peer]:
        pl.semaphore_signal(barrier, inc=1, device_id={"ctx": c}, device_id_type=MESH)

    load = pltpu.make_async_copy(tokens, own, load_sem)
    load.start()
    for i, w in enumerate((w_query, w_key, w_value)):
        pltpu.make_async_copy(w, weights.at[:, pl.ds(DK * i, DK)], w_sem.at[0]).start()
    w_loads = [
        pltpu.make_async_copy(weights, weights, w_sem.at[0]),
        pltpu.make_async_copy(w_beta_in, w_beta, w_sem.at[1]),
        pltpu.make_async_copy(bias_in, bias, w_sem.at[2]),
    ]
    for w in w_loads[1:]:
        w.start()
    pl.semaphore_wait(barrier, len(z_offs) + 7)

    def tree_copies(tree, first, slots, send, recv):
        order, parent = tree

        def copy(o):
            p = parent[o]
            target = head_at(o - p)
            if o in (8, -8):
                rows = pl.ds(0 if o > 0 else ROWS // 2, ROWS // 2)
            else:
                rows = pl.ds(0, ROWS)
            return pltpu.make_async_remote_copy(
                src_ref=first.at[rows] if p == 0 else slots.at[p % NZ, rows],
                dst_ref=slots.at[o % NZ, rows],
                send_sem=send,
                recv_sem=recv.at[0 if o == -8 else o % NZ],
                device_id={"head": target},
                device_id_type=MESH,
            )

        kids = {}
        for o in order:
            kids.setdefault(parent[o], []).append(o)
        return order, copy, kids

    order_a, a_copy, a_kids = tree_copies(TREE_A, tokens, tok, a_send, a_recv)
    for o in a_kids[0]:
        a_copy(o).start()
    for c in x_peers:
        pl.semaphore_signal(hello.at[0], inc=1, device_id={"ctx": c}, device_id_type=MESH)
    for off in (2, -2):
        pl.semaphore_signal(hello.at[1], inc=1, device_id={"head": head_at(off)}, device_id_type=MESH)

    row_tile = pl.multiple_of((chip // 2) * 16, 16)
    col_tile = pl.multiple_of(lax.rem(chip, 2) * 128, 128)
    half = lax.rem(core + z, 2)

    def tile_of(parity, index):
        return wo.at[parity, index, pl.ds(row_tile, 16), pl.ds(col_tile, 128)]

    def w1_copy(off):
        target = head_at(-off)
        return pltpu.make_async_remote_copy(
            src_ref=w_out.at[
                pl.ds(row_tile, 16), pl.ds(pl.multiple_of(target * FEAT + col_tile, 128), 128)
            ],
            dst_ref=tile_of(lax.rem(z, 2), z // 2),
            send_sem=w1_send,
            recv_sem=w1_recv,
            device_id={"head": target},
            device_id_type=MESH,
        )

    w1_mine = pltpu.make_async_copy(
        w_out.at[pl.ds(row_tile, 16), pl.ds(pl.multiple_of(z * FEAT + col_tile, 128), 128)],
        tile_of(lax.rem(z, 2), z // 2),
        w1_own,
    )

    @pl.when(core == 0)
    def _():
        w1_mine.start()

    for w in w_loads:
        w.wait()
    for i in range(NZ):
        wb32[i : i + 1, :] = w_beta[:, i * FEAT : (i + 1) * FEAT].astype(F32)

    def project(block, off, first):
        owner = head_at(-off)
        rows = pl.ds(pl.multiple_of(owner * FEAT, FEAT), FEAT)
        part = dot(block, weights[rows, :])
        beta = block.astype(F32) * wb32[pl.ds(owner, 1), :]
        if first:
            acc[...] = part
            accb[...] = beta
        else:
            acc[...] += part
            accb[...] += beta

    def bytes_of(ref, send, recv):
        return pltpu.make_async_remote_copy(
            src_ref=ref, dst_ref=ref, send_sem=send, recv_sem=recv,
            device_id={"ctx": peer}, device_id_type=MESH,
        )

    w1_counts = (NZ // 2 - 1, NZ // 2)

    def w1_bytes(count):
        return bytes_of(wo.at[0, pl.ds(0, count), pl.ds(0, 16), pl.ds(0, 128)], w1_send, w1_recv)

    w2_bytes = bytes_of(weights.at[pl.ds(0, 640)], w2_send, w2_recv)

    def w2_copy(d):
        target = lax.rem(chip + d, CHIPS)
        tiles = wo.at[half, :, pl.ds(row_tile, 16), pl.ds(col_tile, 128)]
        return pltpu.make_async_remote_copy(
            src_ref=tiles, dst_ref=tiles, send_sem=w2_send, recv_sem=w2_recv,
            device_id={"ctx": target * 2 + core}, device_id_type=MESH,
        )

    load.wait()
    project(own[...], 0, True)
    pl.semaphore_wait(hello.at[1], 2)
    for off in (4, -4):
        pl.semaphore_signal(hello.at[2], inc=1, device_id={"head": head_at(off)}, device_id_type=MESH)
    for step, o in enumerate(order_a):
        a_copy(o).wait_recv()
        for q in a_kids.get(o, ()):
            a_copy(q).start()
        if step == W1_AT:
            pl.semaphore_wait(hello.at[2], 2)
            for q in range(1, NZ):

                @pl.when(core == q % 2)
                def _():
                    w1_copy(q).start()

        if step == W2_AT:
            pl.semaphore_wait(hello.at[0], 3)
            for k in range(2):

                @pl.when(core == k)
                def _():
                    w1_bytes(w1_counts[k]).wait_recv()
                    if k == 0:
                        w1_mine.wait()

            @pl.loop(1, CHIPS)
            def _(d):
                w2_copy(d).start()

        if o != 8:
            project(tok[o % NZ], o, False)

    def unit(m):
        return m / jnp.sqrt(jnp.sum(m * m, axis=1, keepdims=True) + 1e-06)

    query = unit(acc[:, 0:DK])
    key = unit(acc[:, DK : 2 * DK])
    value = acc[:, 2 * DK : 3 * DK]
    beta = jax.nn.sigmoid(jnp.sum(accb[...], axis=1, keepdims=True) + bias[0])
    r = lax.broadcasted_iota(jnp.int32, (ROWS, ROWS), 0)
    c = lax.broadcasted_iota(jnp.int32, (ROWS, ROWS), 1)
    key2 = split(key)
    inner = three(dot_nt, key2, key2)
    inverse = lower_inverse(jnp.where(r > c, beta * inner, 0.0))
    solved = mm3(inverse, jnp.concatenate([beta * key, beta * value], axis=1))
    solved2 = split(solved)
    mine = three(dot_tn, key2, solved2)
    own_x[...] = mine.astype(BF)
    c_copy = pltpu.make_async_remote_copy(
        src_ref=own_x, dst_ref=peer_x, send_sem=c_send, recv_sem=c_recv,
        device_id={"ctx": peer}, device_id_type=MESH,
    )
    c_copy.start()
    causal = jnp.where(r >= c, three(dot_nt, split(query), key2), 0.0)
    seen = three(dot, split(causal), solved2)
    reader_s[...] = query - seen[:, 0:DK]
    local_s[...] = seen[:, DK:]
    c_copy.wait_recv()
    other = peer_x[...].astype(F32)
    early = jnp.where(core == 0, mine, other)
    late = jnp.where(core == 0, other, mine)
    total[...] = (early + late - mm2(late[:, 0:DK].astype(BF), early)).astype(BF)

    mine_rows = pl.ds(pl.multiple_of(core * 64, 64), 64)

    def p_copy(target):
        return pltpu.make_async_remote_copy(
            src_ref=total.at[mine_rows], dst_ref=chain.at[chip, mine_rows],
            send_sem=pf_send.at[0], recv_sem=p_recv.at[chip],
            device_id={"ctx": target * 2 + core}, device_id_type=MESH,
        )

    def p_arrival(source):
        return pltpu.make_async_remote_copy(
            src_ref=total.at[mine_rows], dst_ref=chain.at[source, mine_rows],
            send_sem=pf_send.at[0], recv_sem=p_recv.at[source],
            device_id={"ctx": source * 2 + core}, device_id_type=MESH,
        )

    def f_copy(source):
        return pltpu.make_async_remote_copy(
            src_ref=chain.at[source, mine_rows], dst_ref=chain.at[source, mine_rows],
            send_sem=pf_send.at[1], recv_sem=f_recv.at[source],
            device_id={"ctx": peer}, device_id_type=MESH,
        )

    @pl.loop(0, CHIPS)
    def _(i):
        target = (XS - 1 - i // YS) * YS + lax.rem(y + 6 - lax.rem(i, YS), YS)

        @pl.when(target > chip)
        def _():
            p_copy(target).start()

    state[...] = jnp.zeros_like(state)

    @pl.loop(0, CHIPS - 1 + LAG)
    def _(t):
        @pl.when(t < chip)
        def _():
            p_arrival(t).wait_recv()
            f_copy(t).start()

        @pl.when((t >= LAG) & (t - LAG < chip))
        def _():
            s = t - LAG
            f_copy(s).wait_recv()
            step = chain[s]
            state[...] += step[:, DK:].astype(F32) - mm2(step[:, 0:DK], state[...])

    entry = state[...]
    moved = entry + peer_x[:, DK:].astype(F32) - mm2(peer_x[:, 0:DK], entry)
    entry = jnp.where(core == 0, entry, moved)
    att_own[...] = (local_s[...] + mm3(reader_s[...], entry)).astype(BF)

    order_d, d_copy, d_kids = tree_copies(TREE_D, att_own, att, d_send, d_recv)
    for o in d_kids[0]:
        d_copy(o).start()

    w2_bytes.wait_recv()
    w3_copy = pltpu.make_async_remote_copy(
        src_ref=wo.at[half], dst_ref=wo.at[half], send_sem=w3_send, recv_sem=w3_recv,
        device_id={"ctx": peer}, device_id_type=MESH,
    )
    w3_copy.start()
    w3_arrival = pltpu.make_async_remote_copy(
        src_ref=wo.at[1 - half], dst_ref=wo.at[1 - half], send_sem=w3_send, recv_sem=w3_recv,
        device_id={"ctx": peer}, device_id_type=MESH,
    )
    w3_arrival.wait_recv()

    bytes_of(tok.at[pl.ds(0, NZ - 1)], a_send, a_send).wait_send()
    for k in range(2):

        @pl.when(core == k)
        def _():
            w1_bytes(w1_counts[k]).wait_send()

    w2_bytes.wait_send()
    c_copy.wait_send()

    def chain_bytes(count, send):
        return bytes_of(chain.at[pl.ds(0, count), pl.ds(0, ROWS // 2)], send, send)

    for i in range(CHIPS):

        @pl.when(chip == i)
        def _():
            if i < CHIPS - 1:
                chain_bytes(CHIPS - 1 - i, pf_send.at[0]).wait_send()
            if i > 0:
                chain_bytes(i, pf_send.at[1]).wait_send()


    def columns(off):
        owner = head_at(-off)
        return wo[lax.rem(owner, 2), owner // 2]

    result = dot(att_own[...], columns(0))
    for o in order_d:
        d_copy(o).wait_recv()
        for q in d_kids.get(o, ()):
            d_copy(q).start()
        if o != 8:
            result = result + dot(att[o % NZ], columns(o))
    out[...] = result.astype(BF)

    w3_copy.wait_send()
    bytes_of(att.at[pl.ds(0, NZ - 1)], d_send, d_send).wait_send()


def shards(tokens, w_query, w_key, w_value, w_beta, beta_bias, w_out):
    hbm = pl.BlockSpec(memory_space=pltpu.HBM)
    vmem = pl.BlockSpec(memory_space=pltpu.VMEM)
    dma = pltpu.SemaphoreType.DMA
    return pl.pallas_call(
        kernel,
        out_shape=jax.ShapeDtypeStruct((ROWS, FEAT), BF),
        in_specs=[hbm] * 7,
        out_specs=vmem,
        scratch_shapes=[
            pltpu.VMEM((1, NZ * FEAT), BF),
            pltpu.SMEM((1,), F32),
            pltpu.VMEM((ROWS, FEAT), BF),
            pltpu.VMEM((NZ, ROWS, FEAT), BF),
            pltpu.VMEM((NZ * FEAT, 3 * DK), BF),
            pltpu.VMEM((NZ, FEAT), F32),
            pltpu.VMEM((ROWS, 3 * DK), F32),
            pltpu.VMEM((ROWS, FEAT), F32),
            pltpu.VMEM((2, NZ // 2, ROWS, FEAT), BF),
            pltpu.VMEM((ROWS, 2 * DK), BF),
            pltpu.VMEM((ROWS, 2 * DK), BF),
            pltpu.VMEM((ROWS, 2 * DK), BF),
            pltpu.VMEM((CHIPS, ROWS, 2 * DK), BF),
            pltpu.VMEM((DK, DK), F32),
            pltpu.VMEM((ROWS, DK), BF),
            pltpu.VMEM((NZ, ROWS, DK), BF),
            pltpu.VMEM((ROWS, DK), F32),
            pltpu.VMEM((ROWS, DK), F32),
            dma, dma((3,)), dma, dma((NZ,)), dma, dma, dma, dma, dma, dma, dma,
            dma, dma, dma((2,)), dma((CHIPS,)), dma((CHIPS,)), dma, dma((NZ,)),
            pltpu.SemaphoreType.REGULAR((3,)),
        ],
        compiler_params=pltpu.CompilerParams(
            collective_id=0, has_side_effects=True, vmem_limit_bytes=63 * 2**20
        ),
    )(tokens, w_query, w_key, w_value, w_beta.T, beta_bias, w_out)


def solution(mesh):
    in_specs = (
        P("ctx", "head"),
        P(None, "head"),
        P(None, "head"),
        P(None, "head"),
        P(None, "head"),
        P("head"),
        P("head", None),
    )
    return jax.shard_map(
        shards, mesh=mesh, in_specs=in_specs, out_specs=P("ctx", "head"), check_vma=False
    )
```
